32 devices in a mesh: aperture: 4 (over y, x), tile: 8 (over z, core).
Axes of the slice: x: 2, y: 2, z: 4, core: 2. Of those that a mesh axis runs over, the one named last changes fastest.
Arguments:
- sectors: bfloat16 [4, 96, 512, 2, 512], P('aperture', 'tile'), may hold values from -6 to 6
- footprint: int32 [4, 96, 2], P('aperture', 'tile'), may hold values from 0 to 6, as said below
- own_blocks: bfloat16 [6, 512, 512], replicated, may hold values from -0.25 to 0.25
- edge_blocks: bfloat16 [6, 128, 512], replicated, may hold values from -0.25 to 0.25
- edges: int32 [512, 2], P(('aperture', 'tile')), may hold values from 0 to 4096, as said below
Outputs:
- image: float32 [2, 512, 4096], P(None, ('aperture', 'tile'))
The draws below stay inside these ranges and needn't reach their ends.
Inputs may be any that keep to these rules, and one draw needn't show every extreme that they name: `footprint`: per device, each group's 12 slots at one tile position hold first the live slots (own entry below 6), then dead ones with both entries 6; at least one slot is live; in every draw some device has all 12 slots live. The edge entry is 6 for every slot at the last tile position. `edges`: each interval spans at least 64 cells; in every draw some line starts at 0 and some line ends at 4096.
All inputs are finite; a program needn't handle non-finite values.
Results may differ from the reference program's by a relative error of at most 0.0003.
Values sent between devices are 32-bit elements; how exact they have to be, the bound alone decides.
A program may use at most 128 MiB of HBM per device.

```python
import jax
import jax.numpy as jnp
from jax import lax

TK = 512
KY = 512
SK = 512
HB = 128
NB = 6
GORDER = 8
GMIN = 64
S_DEV = 12
GROUPS = 4
TILES = 8
SLOTS = 96
NX = 4096


def draw_footprint(key, part):
    keys = jax.random.split(key, 5)
    base = jax.random.randint(keys[0], (GROUPS, TILES), 1, 3)
    heavy = jax.random.randint(keys[1], (GROUPS, TILES), 0, 8) == 0
    chosen = jax.random.randint(keys[2], (), 0, GROUPS * TILES)
    device = jnp.arange(GROUPS * TILES, dtype=jnp.int32).reshape(GROUPS, TILES)
    live = jnp.where(heavy | (device == chosen), S_DEV, base)
    slot = jnp.arange(S_DEV, dtype=jnp.int32)
    alive = slot[None, None, :] < live[:, :, None]
    own = jax.random.randint(keys[3], (GROUPS, TILES, S_DEV), 0, NB)
    edge = jax.random.randint(keys[4], (GROUPS, TILES, S_DEV), 0, NB + 1)
    last = jnp.arange(TILES, dtype=jnp.int32)[None, :, None] == TILES - 1
    edge = jnp.where(last, NB, edge)
    own = jnp.where(alive, own, NB)
    edge = jnp.where(alive, edge, NB)
    return jnp.stack([own, edge], -1).reshape(GROUPS, TILES * S_DEV, 2).astype(jnp.int32)


def draw_edges(key, part):
    keys = jax.random.split(key, 4)
    span = jax.random.randint(keys[0], (KY,), GMIN, NX // 4 + 1)
    lower = jax.random.randint(keys[1], (KY,), 0, NX) % (NX - span + 1)
    first = jax.random.randint(keys[2], (), 0, KY)
    second = (first + 1 + jax.random.randint(keys[3], (), 0, KY - 1)) % KY
    rows = jnp.arange(KY, dtype=jnp.int32)
    lower = jnp.where(rows == first, 0, lower)
    lower = jnp.where(rows == second, NX - span, lower)
    return jnp.stack([lower, lower + span], -1).astype(jnp.int32)


def block_levels(rng, shape, shards, low, top_value):
    level, own = 1.0, jax.random.fold_in(rng, 6)
    for axis_at, shards_of in shards:
        draws = jnp.exp(jax.random.uniform(jax.random.fold_in(own, axis_at), (shards_of,), jnp.float32, low / len(shards), top_value / len(shards)))
        level = level * jnp.repeat(draws, shape[axis_at] // shards_of).reshape([-1 if axis == axis_at else 1 for axis in range(len(shape))])
    return level


def centred(key, shape, scale, limit, shards=(), kind=jnp.bfloat16):
    drawn = jax.random.normal(key, shape, jnp.float32) * scale
    if len(shards) > 0:
        drawn = block_levels(key, shape, shards, -0.22, 0.18) * drawn
    return jnp.clip(drawn, min=-limit, max=limit).astype(kind)


def setup_inputs(seed: int = 0) -> dict:
    key_list = jax.random.split(jax.random.key(seed), 6)
    sectors = centred(key_list[0], (GROUPS, SLOTS, SK, 2, KY), 1.0, 6.0, ((0, 4), (1, 8)))
    footprint = draw_footprint(jax.random.fold_in(key_list[5], 71), 0)
    own_blocks = centred(key_list[2], (NB, TK, SK), SK ** -0.5, 0.25)
    edge_blocks = centred(key_list[3], (NB, HB, SK), SK ** -0.5, 0.25)
    edges = draw_edges(jax.random.fold_in(key_list[5], 71), 0)
    return {"sectors": sectors, "footprint": footprint, "own_blocks": own_blocks, "edge_blocks": edge_blocks, "edges": edges}


def gegen_fix(field, edges):
    width = field.shape[-1]
    cells = jnp.arange(width, dtype=jnp.int32)[None, :]
    lower = edges[:, 0:1]
    upper = edges[:, 1:2]
    span = (upper - lower).astype(jnp.float32)
    inside = (cells >= lower) & (cells < upper)
    offset = (cells - lower).astype(jnp.float32)
    xi_vals = jnp.where(inside, -1.0 + (2.0 * offset + 1.0) / span, 0.0)
    base = 1.0 - xi_vals * xi_vals
    weight = jnp.where(inside, base * jnp.sqrt(base), 0.0)
    prev = jnp.ones_like(xi_vals)
    curr = 4.0 * xi_vals
    rebuilt = jnp.zeros_like(field)
    for order in range(GORDER):
        poly = prev if order == 0 else curr
        numer = lax.optimization_barrier(jnp.sum(weight * poly * field, axis=-1))
        denom = lax.optimization_barrier(jnp.sum(weight * poly * poly, axis=-1))
        rebuilt = rebuilt + (numer / denom)[..., None] * poly
        if order >= 1:
            nxt = (2.0 * (order + 2) * xi_vals * curr - (order + 3) * prev) / (order + 1)
            prev, curr = (curr, nxt)
    return jnp.where(inside, rebuilt, field)

def slot_terms(data, foot, own_f, edge_f):
    dims = (((0,), (1,)), ((), ()))

    def step(carry, item):
        total, rim = carry
        block, entry = item
        values = block.astype(jnp.float32)

        def own_term():
            kernel = own_f[jnp.minimum(entry[0], NB - 1)]
            return lax.dot_general(values, kernel, dims, precision=lax.Precision.HIGHEST)

        def edge_term():
            kernel = edge_f[jnp.minimum(entry[1], NB - 1)]
            return lax.dot_general(values, kernel, dims, precision=lax.Precision.HIGHEST)
        total = total + lax.cond(entry[0] < NB, own_term, lambda: jnp.zeros_like(total))
        rim = rim + lax.cond(entry[1] < NB, edge_term, lambda: jnp.zeros_like(rim))
        return ((total, rim), None)
    start = (jnp.zeros((2, KY, TK), jnp.float32), jnp.zeros((2, KY, HB), jnp.float32))
    (total, rim), _ = lax.scan(step, start, (data, foot))
    return (total, rim)

def reference(sectors, footprint, own_blocks, edge_blocks, edges):
    own_f = own_blocks.astype(jnp.float32)
    edge_f = edge_blocks.astype(jnp.float32)
    zero = jnp.zeros((), jnp.int32)

    def visit(flat, grid):
        group = (flat // TILES).astype(jnp.int32)
        place = (flat % TILES).astype(jnp.int32)
        data = lax.dynamic_slice(sectors, (group, place * S_DEV, zero, zero, zero), (1, S_DEV, SK, 2, KY))[0]
        foot = lax.dynamic_slice(footprint, (group, place * S_DEV, zero), (1, S_DEV, 2))[0]
        total, rim = slot_terms(data, foot, own_f, edge_f)
        begin = (place * TK).astype(jnp.int32)
        current = lax.dynamic_slice(grid, (zero, zero, begin), (2, KY, TK))
        grid = lax.dynamic_update_slice(grid, current + total, (zero, zero, begin))
        after = (begin + TK).astype(jnp.int32)
        current = lax.dynamic_slice(grid, (zero, zero, after), (2, KY, HB))
        grid = lax.dynamic_update_slice(grid, current + rim, (zero, zero, after))
        return grid
    grid = jnp.zeros((2, KY, NX + HB), jnp.float32)
    grid = lax.fori_loop(0, GROUPS * TILES, visit, grid)
    grid = grid[:, :, :NX]
    spectrum = lax.complex(grid[0], grid[1])
    pixels = jnp.fft.ifft(spectrum, axis=-1, norm='ortho')
    field = jnp.stack([jnp.real(pixels), jnp.imag(pixels)]).astype(jnp.float32)
    return gegen_fix(field, edges)
```

```python
import functools
import math

import jax
import jax.numpy as jnp
import ml_dtypes
import numpy as np
from jax import lax
from jax.experimental import pallas as pl
from jax.experimental.pallas import tpu as pltpu
from jax.sharding import PartitionSpec as P

GORDER = 8
MESH = pl.DeviceIdType.MESH


def partner(me, step, groups):
    if groups == 4:
        return [3 - me, me + 1 - 2 * lax.rem(me, 2), lax.rem(me + 2, 4)][step - 1]
    return lax.rem(me + step, groups)


def source(me, step, groups):
    if groups == 4:
        return partner(me, step, groups)
    return lax.rem(me + groups - step, groups)


def exchange_kernel(
    groups, tiles, sec_ref, foot_ref, own_hbm, edge_hbm, out_ref,
    held, own_ref, edge_ref, wide, part, arrived, snd, rcv,
    load_sem, kern_sem, rs_send, rs_recv, tr_send, tr_recv,
):
    slots, samples = sec_ref.shape[0], sec_ref.shape[1]
    blocks, cells = own_ref.shape[0], own_ref.shape[1]
    rows, width = part.shape[1], part.shape[2] // 2
    chunks = snd.shape[0]
    piece = rows // chunks
    per = snd.shape[3]
    me = lax.axis_index("aperture")
    tile = lax.axis_index("tile")
    flat = sec_ref.reshape(slots, 2 * samples, sec_ref.shape[3])
    order = [partner(me, step, groups) for step in range(1, groups)] + [me]

    def load(step):
        lanes = pl.ds(pl.multiple_of(order[step] * width, width), width)
        return pltpu.make_async_copy(flat.at[:, :, lanes], held.at[step], load_sem.at[step])

    kernels = [
        pltpu.make_async_copy(own_hbm, own_ref, kern_sem.at[0]),
        pltpu.make_async_copy(edge_hbm, edge_ref, kern_sem.at[1]),
    ]
    for copy in kernels:
        copy.start()
    for step in range(groups):
        load(step).start()

    barrier = pltpu.get_barrier_semaphore()
    for step in range(1, groups):
        pl.semaphore_signal(barrier, inc=1, device_id=(partner(me, step, groups), tile), device_id_type=MESH)
    for step in range(1, tiles):
        pl.semaphore_signal(barrier, inc=1, device_id=(me, lax.rem(tile + step, tiles)), device_id_type=MESH)
    pl.semaphore_wait(barrier, groups + tiles - 2)
    for copy in kernels:
        copy.wait()

    def reduce_copy(step, chunk):
        span = pl.ds(chunk * piece, piece)
        return pltpu.make_async_remote_copy(
            src_ref=part.at[step - 1, span],
            dst_ref=arrived.at[step - 1, span],
            send_sem=rs_send.at[step - 1, chunk],
            recv_sem=rs_recv.at[step - 1, chunk],
            device_id=(partner(me, step, groups), tile),
            device_id_type=MESH,
        )

    for step in range(groups):
        load(step).wait()
        part[step] = jnp.zeros((rows, 2 * width), jnp.float32)

        @pl.loop(0, slots)
        def _(slot):
            wide[...] = held[step, slot].astype(jnp.float32)
            data = jnp.concatenate(
                [wide[pl.ds(0, samples, stride=2), :], wide[pl.ds(1, samples, stride=2), :]], axis=1
            ).astype(jnp.bfloat16)
            own, edge = foot_ref[slot, 0], foot_ref[slot, 1]
            whole = jnp.dot(own_ref[jnp.minimum(own, blocks - 1)], data, preferred_element_type=jnp.float32)
            rim = jnp.dot(edge_ref[jnp.minimum(edge, blocks - 1)], data, preferred_element_type=jnp.float32)
            part[step, :cells] += jnp.where(own < blocks, whole, 0.0)
            part[step, cells:] += jnp.where(edge < blocks, rim, 0.0)

        if step < groups - 1:
            for chunk in range(chunks):
                reduce_copy(step + 1, chunk).start()

    def owner_copy(step, chunk):
        to = lax.rem(tile + step, tiles)
        return pltpu.make_async_remote_copy(
            src_ref=snd.at[chunk, to],
            dst_ref=rcv.at[chunk, tile],
            send_sem=tr_send.at[chunk, step],
            recv_sem=tr_recv.at[chunk, step],
            device_id=(me, to),
            device_id_type=MESH,
        )

    for chunk in range(chunks):
        span = pl.ds(chunk * piece, piece)
        total = part[groups - 1, span]
        for step in range(1, groups):
            reduce_copy(step, chunk).wait_recv()
            total = total + arrived[step - 1, span]
        for p in range(2):
            turned = total[:, p * width:(p + 1) * width].T
            for to in range(tiles):
                snd[chunk, to, p] = turned[to * per:(to + 1) * per]
        for step in range(1, tiles):
            owner_copy(step, chunk).start()
    for chunk in range(chunks):
        out_ref[chunk, tile] = snd[chunk, tile]
    for chunk in range(chunks):
        for step in range(1, tiles):
            copy = owner_copy(step, chunk)
            copy.wait_send()
            copy.wait_recv()
            origin = lax.rem(tile + tiles - step, tiles)
            out_ref[chunk, origin] = rcv[chunk, origin]
    for step in range(1, groups):
        for chunk in range(chunks):
            reduce_copy(step, chunk).wait_send()


def exchange(data, foot, own_blocks, edge_blocks):
    groups, tiles = lax.axis_size("aperture"), lax.axis_size("tile")
    slots, samples, _, lines = data.shape
    cells, extra = own_blocks.shape[1], edge_blocks.shape[1]
    rows, width, piece = cells + extra, lines // groups, extra
    chunks, per = rows // piece, lines // (groups * tiles)
    out = (chunks, tiles, 2, per, piece)
    vmem = pl.BlockSpec(memory_space=pltpu.VMEM)
    hbm = pl.BlockSpec(memory_space=pl.ANY)
    return pl.pallas_call(
        functools.partial(exchange_kernel, groups, tiles),
        out_shape=jax.ShapeDtypeStruct(out, jnp.float32),
        in_specs=[hbm, pl.BlockSpec(memory_space=pltpu.SMEM), hbm, hbm],
        out_specs=vmem,
        scratch_shapes=[
            pltpu.VMEM((groups, slots, 2 * samples, width), jnp.bfloat16),
            pltpu.VMEM(own_blocks.shape, jnp.bfloat16),
            pltpu.VMEM(edge_blocks.shape, jnp.bfloat16),
            pltpu.VMEM((2 * samples, width), jnp.float32),
            pltpu.VMEM((groups, rows, 2 * width), jnp.float32),
            pltpu.VMEM((groups - 1, rows, 2 * width), jnp.float32),
            pltpu.VMEM(out, jnp.float32),
            pltpu.VMEM(out, jnp.float32),
            pltpu.SemaphoreType.DMA((groups,)),
            pltpu.SemaphoreType.DMA((2,)),
            pltpu.SemaphoreType.DMA((groups - 1, chunks)),
            pltpu.SemaphoreType.DMA((groups - 1, chunks)),
            pltpu.SemaphoreType.DMA((chunks, tiles)),
            pltpu.SemaphoreType.DMA((chunks, tiles)),
        ],
        compiler_params=pltpu.CompilerParams(
            collective_id=0, has_side_effects=True, vmem_limit_bytes=48 * 1024 * 1024
        ),
    )(data, foot, own_blocks, edge_blocks)


def split(value):
    high = value.astype(jnp.bfloat16)
    return high, (value - high.astype(jnp.float32)).astype(jnp.bfloat16)


def image_kernel(
    tiles, grid_ref, edges_ref, twist_ref, inner_high, inner_low, place_ref, out_ref
):
    per = edges_ref.shape[0]
    chunks, piece = grid_ref.shape[0], grid_ref.shape[4]
    inner = (chunks - 1) * piece
    real, imag = [], []
    for t in range(tiles):
        for p, into in ((0, real), (1, imag)):
            first = grid_ref[0, t, p]
            if t > 0:
                first = first + grid_ref[chunks - 1, t - 1, p]
            into.append(jnp.concatenate([first] + [grid_ref[c, t, p] for c in range(1, chunks - 1)], axis=1))
    h_real, h_imag = [], []
    for q in range(tiles):
        g_real, g_imag = real[0], imag[0]
        for t in range(1, tiles):
            angle = 2.0 * math.pi * (t * q % tiles) / tiles
            c, s = math.cos(angle), math.sin(angle)
            for factor, re, im in ((c, real[t], imag[t]), (s, -imag[t], real[t])):
                if abs(factor) < 1e-12:
                    continue
                if abs(abs(factor) - 1.0) < 1e-12:
                    g_real = g_real + re if factor > 0 else g_real - re
                    g_imag = g_imag + im if factor > 0 else g_imag - im
                else:
                    g_real = g_real + factor * re
                    g_imag = g_imag + factor * im
        c, s = twist_ref[0, q:q + 1, :], twist_ref[1, q:q + 1, :]
        h_real.append(g_real * c - g_imag * s)
        h_imag.append(g_real * s + g_imag * c)
    stacked = jnp.concatenate(h_real + h_imag, axis=0)
    high, low = split(stacked)
    both = jnp.concatenate([high, low], axis=0)
    dot = functools.partial(jnp.dot, preferred_element_type=jnp.float32)
    count = tiles * per

    def times(index):
        wide = dot(both, inner_high[index])
        return wide[:2 * count] + wide[2 * count:] + dot(high, inner_low[index])

    by_cos, by_sin = times(0), times(1)
    z_real = (by_cos[:count] - by_sin[count:]).reshape(tiles, per, inner)
    z_imag = (by_sin[:count] + by_cos[count:]).reshape(tiles, per, inner)

    lower = edges_ref[:, 0:1][None]
    upper = edges_ref[:, 1:2][None]
    shape = (tiles, per, inner)
    cells = lax.broadcasted_iota(jnp.int32, shape, 2) * tiles + lax.broadcasted_iota(jnp.int32, shape, 0)
    inside = (cells >= lower) & (cells < upper)
    span = (upper - lower).astype(jnp.float32)
    offset = (cells - lower).astype(jnp.float32)
    xi = jnp.where(inside, -1.0 + (2.0 * offset + 1.0) / span, 0.0)
    base = 1.0 - xi * xi
    weight = jnp.where(inside, base * jnp.sqrt(base), 0.0)

    def over_line(value):
        return jnp.sum(jnp.sum(value, axis=0), axis=-1, keepdims=True)[None]

    prev, curr = jnp.ones_like(xi), 4.0 * xi
    re_fix, im_fix = jnp.zeros_like(xi), jnp.zeros_like(xi)
    for order in range(GORDER):
        poly = prev if order == 0 else curr
        weighted = weight * poly
        denom = over_line(weighted * poly)
        re_fix = re_fix + (over_line(weighted * z_real) / denom) * poly
        im_fix = im_fix + (over_line(weighted * z_imag) / denom) * poly
        if order >= 1:
            nxt = xi * curr * (2.0 * (order + 2) / (order + 1)) - prev * ((order + 3) / (order + 1))
            prev, curr = curr, nxt
    fixed = (jnp.where(inside, re_fix, z_real), jnp.where(inside, im_fix, z_imag))

    lanes = 128
    strips = inner // lanes
    lines = []
    for strip in range(strips):
        for value in fixed:
            lines.append(
                jnp.concatenate([value[q, :, strip * lanes:(strip + 1) * lanes] for q in range(tiles)], axis=1)
            )
    high, low = split(jnp.concatenate(lines, axis=0))
    placed = dot(jnp.concatenate([high, low], axis=0), place_ref[...])
    placed = placed[:strips * 2 * per] + placed[strips * 2 * per:]
    for strip in range(strips):
        for p in range(2):
            at = (strip * 2 + p) * per
            out_ref[p, :, strip * lanes * tiles:(strip + 1) * lanes * tiles] = placed[at:at + per]


def tables(tiles, inner):
    width = tiles * inner
    twist = 2.0 * np.pi * np.outer(np.arange(tiles), np.arange(inner)) / width
    twist = np.stack([np.cos(twist), np.sin(twist)]) / math.sqrt(width)
    angle = 2.0 * np.pi * (np.outer(np.arange(inner), np.arange(inner)) % inner) / inner
    table = np.stack([np.cos(angle), np.sin(angle)]).astype(np.float32)
    high = table.astype(ml_dtypes.bfloat16)
    low = (table - high.astype(np.float32)).astype(ml_dtypes.bfloat16)
    lanes = 128
    place = np.zeros((tiles, lanes, lanes * tiles), np.float32)
    for q in range(tiles):
        place[q, np.arange(lanes), np.arange(lanes) * tiles + q] = 1.0
    place = place.reshape(tiles * lanes, lanes * tiles).astype(ml_dtypes.bfloat16)
    return twist.astype(np.float32), high, low, place


def form_image(grid, edges):
    chunks, tiles, _, per, piece = grid.shape
    inner = (chunks - 1) * piece
    twist, high, low, place = tables(tiles, inner)
    vmem = pl.BlockSpec(memory_space=pltpu.VMEM)
    return pl.pallas_call(
        functools.partial(image_kernel, tiles),
        out_shape=jax.ShapeDtypeStruct((2, per, tiles * inner), jnp.float32),
        in_specs=[vmem] * 6,
        out_specs=vmem,
        compiler_params=pltpu.CompilerParams(vmem_limit_bytes=40 * 1024 * 1024),
    )(grid, edges, twist, high, low, place)


def gegen_fix(field, edges):
    width = field.shape[-1]
    cells = jnp.arange(width, dtype=jnp.int32)[None, :]
    lower = edges[:, 0:1]
    upper = edges[:, 1:2]
    span = (upper - lower).astype(jnp.float32)
    inside = (cells >= lower) & (cells < upper)
    offset = (cells - lower).astype(jnp.float32)
    xi_vals = jnp.where(inside, -1.0 + (2.0 * offset + 1.0) / span, 0.0)
    base = 1.0 - xi_vals * xi_vals
    weight = jnp.where(inside, base * jnp.sqrt(base), 0.0)
    prev = jnp.ones_like(xi_vals)
    curr = 4.0 * xi_vals
    rebuilt = jnp.zeros_like(field)
    for order in range(GORDER):
        poly = prev if order == 0 else curr
        numer = jnp.sum(weight * poly * field, axis=-1)
        denom = jnp.sum(weight * poly * poly, axis=-1)
        rebuilt = rebuilt + (numer / denom)[..., None] * poly
        if order >= 1:
            nxt = (2.0 * (order + 2) * xi_vals * curr - (order + 3) * prev) / (order + 1)
            prev, curr = (curr, nxt)
    return jnp.where(inside, rebuilt, field)


def phase_table(first, second, modulus):
    left = jnp.arange(first, dtype=jnp.int32)[:, None]
    right = jnp.arange(second, dtype=jnp.int32)[None, :]
    angle = 2.0 * math.pi / modulus * (left * right % modulus).astype(jnp.float32)
    return (jnp.cos(angle), jnp.sin(angle))


def spectral(field, tiles):
    lines = field.shape[1]
    width = field.shape[2]
    inner = width // tiles
    blocks = field.reshape(2, lines, tiles, inner)
    real_part, imag_part = (blocks[0], blocks[1])
    best = lax.Precision.HIGHEST
    cos_outer, sin_outer = phase_table(tiles, tiles, tiles)
    g_real = jnp.einsum("pt,ctm->cpm", cos_outer, real_part, precision=best) - jnp.einsum(
        "pt,ctm->cpm", sin_outer, imag_part, precision=best
    )
    g_imag = jnp.einsum("pt,ctm->cpm", sin_outer, real_part, precision=best) + jnp.einsum(
        "pt,ctm->cpm", cos_outer, imag_part, precision=best
    )
    cos_twist, sin_twist = phase_table(tiles, inner, width)
    h_real = g_real * cos_twist - g_imag * sin_twist
    h_imag = g_real * sin_twist + g_imag * cos_twist
    cos_inner, sin_inner = phase_table(inner, inner, inner)
    z_real = jnp.einsum("qm,cpm->cqp", cos_inner, h_real, precision=best) - jnp.einsum(
        "qm,cpm->cqp", sin_inner, h_imag, precision=best
    )
    z_imag = jnp.einsum("qm,cpm->cqp", sin_inner, h_real, precision=best) + jnp.einsum(
        "qm,cpm->cqp", cos_inner, h_imag, precision=best
    )
    scale = 1.0 / math.sqrt(width)
    return jnp.stack([z_real, z_imag]).reshape(2, lines, width) * scale


def form_image_wide(grid, edges):
    chunks, tiles, _, per, piece = grid.shape
    inner = (chunks - 1) * piece
    first = grid[0] + jnp.pad(grid[-1, :-1], ((1, 0), (0, 0), (0, 0), (0, 0)))
    blocks = jnp.concatenate([first[None], grid[1:-1]], axis=0)
    field = blocks.transpose(2, 3, 1, 0, 4).reshape(2, per, tiles * inner)
    return gegen_fix(spectral(field, tiles), edges)


def on_device(sectors, footprint, own_blocks, edge_blocks, edges):
    grid = exchange(sectors[0], footprint[0], own_blocks, edge_blocks)
    if grid.shape[1] <= 8 and grid.shape[3] % 8 == 0:
        return form_image(grid, edges)
    return form_image_wide(grid, edges)


def solution(mesh):
    in_specs = (
        P("aperture", "tile", None, None, None),
        P("aperture", "tile", None),
        P(),
        P(),
        P(("aperture", "tile"), None),
    )
    out_specs = P(None, ("aperture", "tile"), None)
    return jax.shard_map(
        on_device, mesh=mesh, in_specs=in_specs, out_specs=out_specs, check_vma=False
    )
```

```python
import functools
import math

import jax
import jax.numpy as jnp
import ml_dtypes
import numpy as np
from jax import lax
from jax.experimental import pallas as pl
from jax.experimental.pallas import tpu as pltpu
from jax.sharding import PartitionSpec as P

GORDER = 8
MESH = pl.DeviceIdType.MESH


def partners(me, groups):
    if groups == 4:
        return [3 - me, lax.rem(me + 2, 4), me + 1 - 2 * lax.rem(me, 2)]
    return [lax.rem(me + step, groups) for step in range(1, groups)]


def exchange_kernel(
    groups, tiles, sec_ref, foot_ref, own_hbm, edge_hbm, out_ref,
    held, own_ref, edge_ref, wide, part, rims, rims_in, arrived, snd, rcv,
    load_sem, kern_sem, rim_send, rim_recv, rs_send, rs_recv, tr_send, tr_recv,
):
    slots, samples = sec_ref.shape[0], sec_ref.shape[1]
    blocks, piece = edge_ref.shape[0], edge_ref.shape[1]
    rows, width = part.shape[1], part.shape[2] // 2
    chunks = snd.shape[0]
    per = snd.shape[3]
    square = groups == 4
    me = lax.axis_index("aperture")
    tile = lax.axis_index("tile")
    flat = sec_ref.reshape(slots, 2 * samples, sec_ref.shape[3])
    others = partners(me, groups)
    order = others + [me]
    last = groups - 1

    def load(step):
        lanes = pl.ds(pl.multiple_of(order[step] * width, width), width)
        return pltpu.make_async_copy(flat.at[:, :, lanes], held.at[step], load_sem.at[step])

    kernels = [
        pltpu.make_async_copy(own_hbm, own_ref, kern_sem.at[0]),
        pltpu.make_async_copy(edge_hbm, edge_ref, kern_sem.at[1]),
    ]
    for copy in kernels:
        copy.start()
    for step in range(groups):
        load(step).start()

    barrier = pltpu.get_barrier_semaphore()
    greeted = others[1:] if square else others
    for other in greeted:
        pl.semaphore_signal(barrier, inc=1, device_id=(other, tile), device_id_type=MESH)
    for step in range(1, tiles):
        pl.semaphore_signal(barrier, inc=1, device_id=(me, lax.rem(tile + step, tiles)), device_id_type=MESH)
    pl.semaphore_wait(barrier, len(greeted) + tiles - 1)
    for copy in kernels:
        copy.wait()

    def span(chunk):
        return pl.ds(chunk * piece, piece)

    def rim_copy(step):
        return pltpu.make_async_remote_copy(
            src_ref=rims.at[step],
            dst_ref=rims_in.at[step],
            send_sem=rim_send.at[step],
            recv_sem=rim_recv.at[step],
            device_id=(me, lax.rem(tile + 1, tiles)),
            device_id_type=MESH,
        )

    def add_rim(step):
        @pl.when(tile > 0)
        def _():
            rim_copy(step).wait_recv()
            part[step, :piece] += rims_in[step]

    def reduce_copy(step, chunk):
        to = others[step]
        if square and step == 0:
            to = others[2 if chunk % 2 else 1]
        return pltpu.make_async_remote_copy(
            src_ref=part.at[step, span(chunk)],
            dst_ref=arrived.at[step, span(chunk)],
            send_sem=rs_send.at[step, chunk],
            recv_sem=rs_recv.at[step, chunk],
            device_id=(to, tile),
            device_id_type=MESH,
        )

    def relay(step, chunk):
        reduce_copy(0, chunk).wait_recv()
        part[step, span(chunk)] += arrived[0, span(chunk)]
        reduce_copy(step, chunk).start()

    for step in range(groups):
        load(step).wait()
        part[step] = jnp.zeros((rows, 2 * width), jnp.float32)
        rims[step] = jnp.zeros((piece, 2 * width), jnp.float32)

        @pl.loop(0, slots)
        def _(slot):
            wide[...] = held[step, slot].astype(jnp.float32)
            data = jnp.concatenate(
                [wide[pl.ds(0, samples, stride=2), :], wide[pl.ds(1, samples, stride=2), :]], axis=1
            ).astype(jnp.bfloat16)
            own, edge = foot_ref[slot, 0], foot_ref[slot, 1]
            whole = jnp.dot(own_ref[jnp.minimum(own, blocks - 1)], data, preferred_element_type=jnp.float32)
            rim = jnp.dot(edge_ref[jnp.minimum(edge, blocks - 1)], data, preferred_element_type=jnp.float32)
            part[step] += jnp.where(own < blocks, whole, 0.0)
            rims[step] += jnp.where(edge < blocks, rim, 0.0)

        @pl.when(tile < tiles - 1)
        def _():
            rim_copy(step).start()

        if not square:
            if step > 0:
                add_rim(step - 1)
                reduce_copy(step - 1, 0).start()
            if step < last:
                for chunk in range(1, chunks):
                    reduce_copy(step, chunk).start()
        elif step == 0:
            for chunk in range(1, chunks):
                reduce_copy(0, chunk).start()
        elif step == 1:
            add_rim(0)
            reduce_copy(0, 0).start()
            for chunk in range(2, chunks, 2):
                reduce_copy(1, chunk).start()
        elif step == 2:
            for chunk in range(1, chunks, 2):
                reduce_copy(2, chunk).start()
            for chunk in range(1, chunks, 2):
                relay(1, chunk)
            add_rim(1)
            reduce_copy(1, 0).start()
        else:
            for chunk in range(2, chunks, 2):
                relay(2, chunk)
            add_rim(2)
            relay(2, 0)

    def owner_copy(step, chunk):
        to = lax.rem(tile + step, tiles)
        return pltpu.make_async_remote_copy(
            src_ref=snd.at[chunk, to],
            dst_ref=rcv.at[chunk, tile],
            send_sem=tr_send.at[chunk, step],
            recv_sem=tr_recv.at[chunk, step],
            device_id=(me, to),
            device_id_type=MESH,
        )

    turn = list(range(1, chunks, 2)) + list(range(2, chunks, 2)) + [0]
    for chunk in turn:
        if chunk == 0:
            add_rim(last)
        total = part[last, span(chunk)]
        for step in range(1 if square else 0, last):
            reduce_copy(step, chunk).wait_recv()
            total = total + arrived[step, span(chunk)]
        for p in range(2):
            turned = total[:, p * width:(p + 1) * width].T
            for to in range(tiles):
                snd[chunk, to, p] = turned[to * per:(to + 1) * per]
        for step in range(1, tiles):
            owner_copy(step, chunk).start()
    for chunk in range(chunks):
        out_ref[chunk, tile] = snd[chunk, tile]
    for chunk in turn:
        for step in range(1, tiles):
            copy = owner_copy(step, chunk)
            copy.wait_send()
            copy.wait_recv()
            origin = lax.rem(tile + tiles - step, tiles)
            out_ref[chunk, origin] = rcv[chunk, origin]
    for step in range(last):
        for chunk in range(chunks):
            reduce_copy(step, chunk).wait_send()

    @pl.when(tile < tiles - 1)
    def _():
        for step in range(groups):
            rim_copy(step).wait_send()


def exchange(data, foot, own_blocks, edge_blocks):
    groups, tiles = lax.axis_size("aperture"), lax.axis_size("tile")
    slots, samples, _, lines = data.shape
    rows, piece = own_blocks.shape[1], edge_blocks.shape[1]
    width = lines // groups
    chunks, per = rows // piece, lines // (groups * tiles)
    out = (chunks, tiles, 2, per, piece)
    vmem = pl.BlockSpec(memory_space=pltpu.VMEM)
    hbm = pl.BlockSpec(memory_space=pl.ANY)
    return pl.pallas_call(
        functools.partial(exchange_kernel, groups, tiles),
        out_shape=jax.ShapeDtypeStruct(out, jnp.float32),
        in_specs=[hbm, pl.BlockSpec(memory_space=pltpu.SMEM), hbm, hbm],
        out_specs=vmem,
        scratch_shapes=[
            pltpu.VMEM((groups, slots, 2 * samples, width), jnp.bfloat16),
            pltpu.VMEM(own_blocks.shape, jnp.bfloat16),
            pltpu.VMEM(edge_blocks.shape, jnp.bfloat16),
            pltpu.VMEM((2 * samples, width), jnp.float32),
            pltpu.VMEM((groups, rows, 2 * width), jnp.float32),
            pltpu.VMEM((groups, piece, 2 * width), jnp.float32),
            pltpu.VMEM((groups, piece, 2 * width), jnp.float32),
            pltpu.VMEM((groups - 1, rows, 2 * width), jnp.float32),
            pltpu.VMEM(out, jnp.float32),
            pltpu.VMEM(out, jnp.float32),
            pltpu.SemaphoreType.DMA((groups,)),
            pltpu.SemaphoreType.DMA((2,)),
            pltpu.SemaphoreType.DMA((groups,)),
            pltpu.SemaphoreType.DMA((groups,)),
            pltpu.SemaphoreType.DMA((groups - 1, chunks)),
            pltpu.SemaphoreType.DMA((groups - 1, chunks)),
            pltpu.SemaphoreType.DMA((chunks, tiles)),
            pltpu.SemaphoreType.DMA((chunks, tiles)),
        ],
        compiler_params=pltpu.CompilerParams(
            collective_id=0, has_side_effects=True, vmem_limit_bytes=48 * 1024 * 1024
        ),
    )(data, foot, own_blocks, edge_blocks)


def split(value):
    high = value.astype(jnp.bfloat16)
    return high, (value - high.astype(jnp.float32)).astype(jnp.bfloat16)


def image_kernel(
    tiles, grid_ref, edges_ref, twist_ref, inner_high, inner_low, place_ref, out_ref
):
    per = edges_ref.shape[0]
    chunks, piece = grid_ref.shape[0], grid_ref.shape[4]
    inner = chunks * piece
    real, imag = [], []
    for t in range(tiles):
        for p, into in ((0, real), (1, imag)):
            into.append(jnp.concatenate([grid_ref[c, t, p] for c in range(chunks)], axis=1))
    h_real, h_imag = [], []
    for q in range(tiles):
        g_real, g_imag = real[0], imag[0]
        for t in range(1, tiles):
            angle = 2.0 * math.pi * (t * q % tiles) / tiles
            c, s = math.cos(angle), math.sin(angle)
            for factor, re, im in ((c, real[t], imag[t]), (s, -imag[t], real[t])):
                if abs(factor) < 1e-12:
                    continue
                if abs(abs(factor) - 1.0) < 1e-12:
                    g_real = g_real + re if factor > 0 else g_real - re
                    g_imag = g_imag + im if factor > 0 else g_imag - im
                else:
                    g_real = g_real + factor * re
                    g_imag = g_imag + factor * im
        c, s = twist_ref[0, q:q + 1, :], twist_ref[1, q:q + 1, :]
        h_real.append(g_real * c - g_imag * s)
        h_imag.append(g_real * s + g_imag * c)
    stacked = jnp.concatenate(h_real + h_imag, axis=0)
    high, low = split(stacked)
    both = jnp.concatenate([high, low], axis=0)
    dot = functools.partial(jnp.dot, preferred_element_type=jnp.float32)
    count = tiles * per

    def times(index):
        wide = dot(both, inner_high[index])
        return wide[:2 * count] + wide[2 * count:] + dot(high, inner_low[index])

    by_cos, by_sin = times(0), times(1)
    z_real = (by_cos[:count] - by_sin[count:]).reshape(tiles, per, inner)
    z_imag = (by_sin[:count] + by_cos[count:]).reshape(tiles, per, inner)

    lower = edges_ref[:, 0:1][None]
    upper = edges_ref[:, 1:2][None]
    shape = (tiles, per, inner)
    cells = lax.broadcasted_iota(jnp.int32, shape, 2) * tiles + lax.broadcasted_iota(jnp.int32, shape, 0)
    inside = (cells >= lower) & (cells < upper)
    span = (upper - lower).astype(jnp.float32)
    offset = (cells - lower).astype(jnp.float32)
    xi = jnp.where(inside, -1.0 + (2.0 * offset + 1.0) / span, 0.0)
    base = 1.0 - xi * xi
    weight = jnp.where(inside, base * jnp.sqrt(base), 0.0)

    def over_line(value):
        return jnp.sum(jnp.sum(value, axis=0), axis=-1, keepdims=True)[None]

    prev, curr = jnp.ones_like(xi), 4.0 * xi
    re_fix, im_fix = jnp.zeros_like(xi), jnp.zeros_like(xi)
    for order in range(GORDER):
        poly = prev if order == 0 else curr
        weighted = weight * poly
        denom = over_line(weighted * poly)
        re_fix = re_fix + (over_line(weighted * z_real) / denom) * poly
        im_fix = im_fix + (over_line(weighted * z_imag) / denom) * poly
        if order >= 1:
            nxt = xi * curr * (2.0 * (order + 2) / (order + 1)) - prev * ((order + 3) / (order + 1))
            prev, curr = curr, nxt
    fixed = (jnp.where(inside, re_fix, z_real), jnp.where(inside, im_fix, z_imag))

    lanes = 128
    strips = inner // lanes
    lines = []
    for strip in range(strips):
        for value in fixed:
            lines.append(
                jnp.concatenate([value[q, :, strip * lanes:(strip + 1) * lanes] for q in range(tiles)], axis=1)
            )
    high, low = split(jnp.concatenate(lines, axis=0))
    placed = dot(jnp.concatenate([high, low], axis=0), place_ref[...])
    placed = placed[:strips * 2 * per] + placed[strips * 2 * per:]
    for strip in range(strips):
        for p in range(2):
            at = (strip * 2 + p) * per
            out_ref[p, :, strip * lanes * tiles:(strip + 1) * lanes * tiles] = placed[at:at + per]


def tables(tiles, inner):
    width = tiles * inner
    twist = 2.0 * np.pi * np.outer(np.arange(tiles), np.arange(inner)) / width
    twist = np.stack([np.cos(twist), np.sin(twist)]) / math.sqrt(width)
    angle = 2.0 * np.pi * (np.outer(np.arange(inner), np.arange(inner)) % inner) / inner
    table = np.stack([np.cos(angle), np.sin(angle)]).astype(np.float32)
    high = table.astype(ml_dtypes.bfloat16)
    low = (table - high.astype(np.float32)).astype(ml_dtypes.bfloat16)
    lanes = 128
    place = np.zeros((tiles, lanes, lanes * tiles), np.float32)
    for q in range(tiles):
        place[q, np.arange(lanes), np.arange(lanes) * tiles + q] = 1.0
    place = place.reshape(tiles * lanes, lanes * tiles).astype(ml_dtypes.bfloat16)
    return twist.astype(np.float32), high, low, place


def form_image(grid, edges):
    chunks, tiles, _, per, piece = grid.shape
    inner = chunks * piece
    twist, high, low, place = tables(tiles, inner)
    vmem = pl.BlockSpec(memory_space=pltpu.VMEM)
    return pl.pallas_call(
        functools.partial(image_kernel, tiles),
        out_shape=jax.ShapeDtypeStruct((2, per, tiles * inner), jnp.float32),
        in_specs=[vmem] * 6,
        out_specs=vmem,
        compiler_params=pltpu.CompilerParams(vmem_limit_bytes=40 * 1024 * 1024),
    )(grid, edges, twist, high, low, place)


def gegen_fix(field, edges):
    width = field.shape[-1]
    cells = jnp.arange(width, dtype=jnp.int32)[None, :]
    lower = edges[:, 0:1]
    upper = edges[:, 1:2]
    span = (upper - lower).astype(jnp.float32)
    inside = (cells >= lower) & (cells < upper)
    offset = (cells - lower).astype(jnp.float32)
    xi_vals = jnp.where(inside, -1.0 + (2.0 * offset + 1.0) / span, 0.0)
    base = 1.0 - xi_vals * xi_vals
    weight = jnp.where(inside, base * jnp.sqrt(base), 0.0)
    prev = jnp.ones_like(xi_vals)
    curr = 4.0 * xi_vals
    rebuilt = jnp.zeros_like(field)
    for order in range(GORDER):
        poly = prev if order == 0 else curr
        numer = jnp.sum(weight * poly * field, axis=-1)
        denom = jnp.sum(weight * poly * poly, axis=-1)
        rebuilt = rebuilt + (numer / denom)[..., None] * poly
        if order >= 1:
            nxt = (2.0 * (order + 2) * xi_vals * curr - (order + 3) * prev) / (order + 1)
            prev, curr = (curr, nxt)
    return jnp.where(inside, rebuilt, field)


def phase_table(first, second, modulus):
    left = jnp.arange(first, dtype=jnp.int32)[:, None]
    right = jnp.arange(second, dtype=jnp.int32)[None, :]
    angle = 2.0 * math.pi / modulus * (left * right % modulus).astype(jnp.float32)
    return (jnp.cos(angle), jnp.sin(angle))


def spectral(field, tiles):
    lines = field.shape[1]
    width = field.shape[2]
    inner = width // tiles
    blocks = field.reshape(2, lines, tiles, inner)
    real_part, imag_part = (blocks[0], blocks[1])
    best = lax.Precision.HIGHEST
    cos_outer, sin_outer = phase_table(tiles, tiles, tiles)
    g_real = jnp.einsum("pt,ctm->cpm", cos_outer, real_part, precision=best) - jnp.einsum(
        "pt,ctm->cpm", sin_outer, imag_part, precision=best
    )
    g_imag = jnp.einsum("pt,ctm->cpm", sin_outer, real_part, precision=best) + jnp.einsum(
        "pt,ctm->cpm", cos_outer, imag_part, precision=best
    )
    cos_twist, sin_twist = phase_table(tiles, inner, width)
    h_real = g_real * cos_twist - g_imag * sin_twist
    h_imag = g_real * sin_twist + g_imag * cos_twist
    cos_inner, sin_inner = phase_table(inner, inner, inner)
    z_real = jnp.einsum("qm,cpm->cqp", cos_inner, h_real, precision=best) - jnp.einsum(
        "qm,cpm->cqp", sin_inner, h_imag, precision=best
    )
    z_imag = jnp.einsum("qm,cpm->cqp", sin_inner, h_real, precision=best) + jnp.einsum(
        "qm,cpm->cqp", cos_inner, h_imag, precision=best
    )
    scale = 1.0 / math.sqrt(width)
    return jnp.stack([z_real, z_imag]).reshape(2, lines, width) * scale


def form_image_wide(grid, edges):
    chunks, tiles, _, per, piece = grid.shape
    inner = chunks * piece
    field = grid.transpose(2, 3, 1, 0, 4).reshape(2, per, tiles * inner)
    return gegen_fix(spectral(field, tiles), edges)


def on_device(sectors, footprint, own_blocks, edge_blocks, edges):
    grid = exchange(sectors[0], footprint[0], own_blocks, edge_blocks)
    if grid.shape[1] <= 8 and grid.shape[3] % 8 == 0:
        return form_image(grid, edges)
    return form_image_wide(grid, edges)


def solution(mesh):
    in_specs = (
        P("aperture", "tile", None, None, None),
        P("aperture", "tile", None),
        P(),
        P(),
        P(("aperture", "tile"), None),
    )
    out_specs = P(None, ("aperture", "tile"), None)
    return jax.shard_map(
        on_device, mesh=mesh, in_specs=in_specs, out_specs=out_specs, check_vma=False
    )
```

```python
import functools
import math

import jax
import jax.numpy as jnp
import ml_dtypes
import numpy as np
from jax import lax
from jax.experimental import pallas as pl
from jax.experimental.pallas import tpu as pltpu
from jax.sharding import PartitionSpec as P

GORDER = 8
MESH = pl.DeviceIdType.MESH


def partners(me, groups):
    if groups == 4:
        return [3 - me, lax.rem(me + 2, 4), me + 1 - 2 * lax.rem(me, 2)]
    return [lax.rem(me + step, groups) for step in range(1, groups)]


def exchange_kernel(
    groups, tiles, sec_ref, foot_ref, own_hbm, edge_hbm, out_ref,
    held, own_ref, edge_ref, wide, part, rims, rims_in, arrived, snd, rcv,
    load_sem, kern_sem, rim_send, rim_recv, rs_send, rs_recv, tr_send, tr_recv,
):
    slots, samples = sec_ref.shape[0], sec_ref.shape[1]
    blocks, piece = edge_ref.shape[0], edge_ref.shape[1]
    rows, width = part.shape[1], part.shape[2] // 2
    chunks = snd.shape[0]
    per = snd.shape[3]
    square = groups == 4
    me = lax.axis_index("aperture")
    tile = lax.axis_index("tile")
    flat = sec_ref.reshape(slots, 2 * samples, sec_ref.shape[3])
    others = partners(me, groups)
    order = others + [me]
    last = groups - 1

    def load(step):
        lanes = pl.ds(pl.multiple_of(order[step] * width, width), width)
        return pltpu.make_async_copy(flat.at[:, :, lanes], held.at[step], load_sem.at[step])

    kernels = [
        pltpu.make_async_copy(own_hbm, own_ref, kern_sem.at[0]),
        pltpu.make_async_copy(edge_hbm, edge_ref, kern_sem.at[1]),
    ]
    for copy in kernels:
        copy.start()
    for step in range(groups):
        load(step).start()

    barrier = pltpu.get_barrier_semaphore()
    greeted = others[1:] if square else others
    for other in greeted:
        pl.semaphore_signal(barrier, inc=1, device_id=(other, tile), device_id_type=MESH)
    for step in range(1, tiles):
        pl.semaphore_signal(barrier, inc=1, device_id=(me, lax.rem(tile + step, tiles)), device_id_type=MESH)
    pl.semaphore_wait(barrier, len(greeted) + tiles - 1)
    for copy in kernels:
        copy.wait()

    def span(chunk):
        return pl.ds(chunk * piece, piece)

    def rim_copy(step):
        return pltpu.make_async_remote_copy(
            src_ref=rims.at[step],
            dst_ref=rims_in.at[step],
            send_sem=rim_send.at[step],
            recv_sem=rim_recv.at[step],
            device_id=(me, lax.rem(tile + 1, tiles)),
            device_id_type=MESH,
        )

    def add_rim(step):
        @pl.when(tile > 0)
        def _():
            rim_copy(step).wait_recv()
            part[step, :piece] += rims_in[step]

    def reduce_copy(step, chunk):
        to = others[step]
        if square and step == 0:
            to = others[2 if chunk % 2 else 1]
        return pltpu.make_async_remote_copy(
            src_ref=part.at[step, span(chunk)],
            dst_ref=arrived.at[step, span(chunk)],
            send_sem=rs_send.at[step, chunk],
            recv_sem=rs_recv.at[step, chunk],
            device_id=(to, tile),
            device_id_type=MESH,
        )

    def relay(step, chunk):
        reduce_copy(0, chunk).wait_recv()
        part[step, span(chunk)] += arrived[0, span(chunk)]
        reduce_copy(step, chunk).start()

    for step in range(groups):
        load(step).wait()
        part[step] = jnp.zeros((rows, 2 * width), jnp.float32)
        rims[step] = jnp.zeros((piece, 2 * width), jnp.float32)

        @pl.loop(0, slots)
        def _(slot):
            wide[...] = held[step, slot].astype(jnp.float32)
            data = jnp.concatenate(
                [wide[pl.ds(0, samples, stride=2), :], wide[pl.ds(1, samples, stride=2), :]], axis=1
            ).astype(jnp.bfloat16)
            own, edge = foot_ref[0, slot], foot_ref[1, slot]
            whole = jnp.dot(own_ref[jnp.minimum(own, blocks - 1)], data, preferred_element_type=jnp.float32)
            rim = jnp.dot(edge_ref[jnp.minimum(edge, blocks - 1)], data, preferred_element_type=jnp.float32)
            part[step] += jnp.where(own < blocks, whole, 0.0)
            rims[step] += jnp.where(edge < blocks, rim, 0.0)

        @pl.when(tile < tiles - 1)
        def _():
            rim_copy(step).start()

        if not square:
            if step > 0:
                add_rim(step - 1)
                reduce_copy(step - 1, 0).start()
            if step < last:
                for chunk in range(1, chunks):
                    reduce_copy(step, chunk).start()
        elif step == 0:
            for chunk in range(1, chunks):
                reduce_copy(0, chunk).start()
        elif step == 1:
            add_rim(0)
            reduce_copy(0, 0).start()
            for chunk in range(2, chunks, 2):
                reduce_copy(1, chunk).start()
        elif step == 2:
            for chunk in range(1, chunks, 2):
                reduce_copy(2, chunk).start()
            for chunk in range(1, chunks, 2):
                relay(1, chunk)
            add_rim(1)
            reduce_copy(1, 0).start()
        else:
            for chunk in range(2, chunks, 2):
                relay(2, chunk)
            add_rim(2)
            relay(2, 0)

    def owner_copy(step, chunk):
        to = lax.rem(tile + step, tiles)
        return pltpu.make_async_remote_copy(
            src_ref=snd.at[chunk, to],
            dst_ref=rcv.at[chunk, tile],
            send_sem=tr_send.at[chunk, step],
            recv_sem=tr_recv.at[chunk, step],
            device_id=(me, to),
            device_id_type=MESH,
        )

    turn = list(range(1, chunks, 2)) + list(range(2, chunks, 2)) + [0]
    for chunk in turn:
        if chunk == 0:
            add_rim(last)
        total = part[last, span(chunk)]
        for step in range(1 if square else 0, last):
            reduce_copy(step, chunk).wait_recv()
            total = total + arrived[step, span(chunk)]
        for p in range(2):
            turned = total[:, p * width:(p + 1) * width].T
            for to in range(tiles):
                snd[chunk, to, p] = turned[to * per:(to + 1) * per]
        for step in range(1, tiles):
            owner_copy(step, chunk).start()
    for chunk in range(chunks):
        out_ref[chunk, tile] = snd[chunk, tile]
    for chunk in turn:
        for step in range(1, tiles):
            copy = owner_copy(step, chunk)
            copy.wait_send()
            copy.wait_recv()
            origin = lax.rem(tile + tiles - step, tiles)
            out_ref[chunk, origin] = rcv[chunk, origin]
    for step in range(last):
        for chunk in range(chunks):
            reduce_copy(step, chunk).wait_send()

    @pl.when(tile < tiles - 1)
    def _():
        for step in range(groups):
            rim_copy(step).wait_send()


def exchange(data, foot, own_blocks, edge_blocks):
    groups, tiles = lax.axis_size("aperture"), lax.axis_size("tile")
    slots, samples, _, lines = data.shape
    rows, piece = own_blocks.shape[1], edge_blocks.shape[1]
    width = lines // groups
    chunks, per = rows // piece, lines // (groups * tiles)
    out = (chunks, tiles, 2, per, piece)
    vmem = pl.BlockSpec(memory_space=pltpu.VMEM)
    hbm = pl.BlockSpec(memory_space=pl.ANY)
    return pl.pallas_call(
        functools.partial(exchange_kernel, groups, tiles),
        out_shape=jax.ShapeDtypeStruct(out, jnp.float32),
        in_specs=[hbm, pl.BlockSpec(memory_space=pltpu.SMEM), hbm, hbm],
        out_specs=vmem,
        scratch_shapes=[
            pltpu.VMEM((groups, slots, 2 * samples, width), jnp.bfloat16),
            pltpu.VMEM(own_blocks.shape, jnp.bfloat16),
            pltpu.VMEM(edge_blocks.shape, jnp.bfloat16),
            pltpu.VMEM((2 * samples, width), jnp.float32),
            pltpu.VMEM((groups, rows, 2 * width), jnp.float32),
            pltpu.VMEM((groups, piece, 2 * width), jnp.float32),
            pltpu.VMEM((groups, piece, 2 * width), jnp.float32),
            pltpu.VMEM((groups - 1, rows, 2 * width), jnp.float32),
            pltpu.VMEM(out, jnp.float32),
            pltpu.VMEM(out, jnp.float32),
            pltpu.SemaphoreType.DMA((groups,)),
            pltpu.SemaphoreType.DMA((2,)),
            pltpu.SemaphoreType.DMA((groups,)),
            pltpu.SemaphoreType.DMA((groups,)),
            pltpu.SemaphoreType.DMA((groups - 1, chunks)),
            pltpu.SemaphoreType.DMA((groups - 1, chunks)),
            pltpu.SemaphoreType.DMA((chunks, tiles)),
            pltpu.SemaphoreType.DMA((chunks, tiles)),
        ],
        compiler_params=pltpu.CompilerParams(
            collective_id=0, has_side_effects=True, vmem_limit_bytes=62 * 1024 * 1024
        ),
    )(data, foot.T, own_blocks, edge_blocks)


def split(value):
    high = value.astype(jnp.bfloat16)
    return high, (value - high.astype(jnp.float32)).astype(jnp.bfloat16)


def image_kernel(
    tiles, grid_ref, edges_ref, twist_ref, high_hbm, low_hbm, place_hbm, out_ref,
    inner_high, inner_low, place_ref, sem,
):
    per = edges_ref.shape[1]
    loads = [
        pltpu.make_async_copy(high_hbm, inner_high, sem.at[0]),
        pltpu.make_async_copy(low_hbm, inner_low, sem.at[1]),
        pltpu.make_async_copy(place_hbm, place_ref, sem.at[2]),
    ]
    for copy in loads:
        copy.start()
    chunks, piece = grid_ref.shape[0], grid_ref.shape[4]
    inner = chunks * piece
    real, imag = [], []
    for t in range(tiles):
        for p, into in ((0, real), (1, imag)):
            into.append(jnp.concatenate([grid_ref[c, t, p] for c in range(chunks)], axis=1))
    h_real, h_imag = [], []
    for q in range(tiles):
        g_real, g_imag = real[0], imag[0]
        for t in range(1, tiles):
            angle = 2.0 * math.pi * (t * q % tiles) / tiles
            c, s = math.cos(angle), math.sin(angle)
            for factor, re, im in ((c, real[t], imag[t]), (s, -imag[t], real[t])):
                if abs(factor) < 1e-12:
                    continue
                if abs(abs(factor) - 1.0) < 1e-12:
                    g_real = g_real + re if factor > 0 else g_real - re
                    g_imag = g_imag + im if factor > 0 else g_imag - im
                else:
                    g_real = g_real + factor * re
                    g_imag = g_imag + factor * im
        c, s = twist_ref[0, q:q + 1, :], twist_ref[1, q:q + 1, :]
        h_real.append(g_real * c - g_imag * s)
        h_imag.append(g_real * s + g_imag * c)
    stacked = jnp.concatenate(h_real + h_imag, axis=0)
    high, low = split(stacked)
    both = jnp.concatenate([high, low], axis=0)
    dot = functools.partial(jnp.dot, preferred_element_type=jnp.float32)
    count = tiles * per

    def times(index):
        wide = dot(both, inner_high[index])
        return wide[:2 * count] + wide[2 * count:] + dot(high, inner_low[index])

    loads[0].wait()
    loads[1].wait()
    by_cos, by_sin = times(0), times(1)
    z_real = (by_cos[:count] - by_sin[count:]).reshape(tiles, per, inner)
    z_imag = (by_sin[:count] + by_cos[count:]).reshape(tiles, per, inner)

    line = lax.broadcasted_iota(jnp.int32, (1, per, 1), 1)
    lower = upper = jnp.zeros((1, per, 1), jnp.int32)
    for at in range(per):
        lower = jnp.where(line == at, edges_ref[0, at], lower)
        upper = jnp.where(line == at, edges_ref[1, at], upper)
    shape = (tiles, per, inner)
    cells = lax.broadcasted_iota(jnp.int32, shape, 2) * tiles + lax.broadcasted_iota(jnp.int32, shape, 0)
    inside = (cells >= lower) & (cells < upper)
    span = (upper - lower).astype(jnp.float32)
    offset = (cells - lower).astype(jnp.float32)
    xi = jnp.where(inside, -1.0 + (2.0 * offset + 1.0) / span, 0.0)
    base = 1.0 - xi * xi
    weight = jnp.where(inside, base * jnp.sqrt(base), 0.0)

    def over_line(value):
        return jnp.sum(jnp.sum(value, axis=0), axis=-1, keepdims=True)[None]

    prev, curr = jnp.ones_like(xi), 4.0 * xi
    re_fix, im_fix = jnp.zeros_like(xi), jnp.zeros_like(xi)
    for order in range(GORDER):
        poly = prev if order == 0 else curr
        weighted = weight * poly
        denom = over_line(weighted * poly)
        re_fix = re_fix + (over_line(weighted * z_real) / denom) * poly
        im_fix = im_fix + (over_line(weighted * z_imag) / denom) * poly
        if order >= 1:
            nxt = xi * curr * (2.0 * (order + 2) / (order + 1)) - prev * ((order + 3) / (order + 1))
            prev, curr = curr, nxt
    fixed = (jnp.where(inside, re_fix, z_real), jnp.where(inside, im_fix, z_imag))

    lanes = 128
    strips = inner // lanes
    lines = []
    for strip in range(strips):
        for value in fixed:
            lines.append(
                jnp.concatenate([value[q, :, strip * lanes:(strip + 1) * lanes] for q in range(tiles)], axis=1)
            )
    high, low = split(jnp.concatenate(lines, axis=0))
    loads[2].wait()
    placed = dot(jnp.concatenate([high, low], axis=0), place_ref[...])
    placed = placed[:strips * 2 * per] + placed[strips * 2 * per:]
    for strip in range(strips):
        for p in range(2):
            at = (strip * 2 + p) * per
            out_ref[p, :, strip * lanes * tiles:(strip + 1) * lanes * tiles] = placed[at:at + per]


def tables(tiles, inner):
    width = tiles * inner
    twist = 2.0 * np.pi * np.outer(np.arange(tiles), np.arange(inner)) / width
    twist = np.stack([np.cos(twist), np.sin(twist)]) / math.sqrt(width)
    angle = 2.0 * np.pi * (np.outer(np.arange(inner), np.arange(inner)) % inner) / inner
    table = np.stack([np.cos(angle), np.sin(angle)]).astype(np.float32)
    high = table.astype(ml_dtypes.bfloat16)
    low = (table - high.astype(np.float32)).astype(ml_dtypes.bfloat16)
    lanes = 128
    place = np.zeros((tiles, lanes, lanes * tiles), np.float32)
    for q in range(tiles):
        place[q, np.arange(lanes), np.arange(lanes) * tiles + q] = 1.0
    place = place.reshape(tiles * lanes, lanes * tiles).astype(ml_dtypes.bfloat16)
    return twist.astype(np.float32), high, low, place


def form_image(grid, edges):
    chunks, tiles, _, per, piece = grid.shape
    inner = chunks * piece
    twist, high, low, place = tables(tiles, inner)
    vmem = pl.BlockSpec(memory_space=pltpu.VMEM)
    hbm = pl.BlockSpec(memory_space=pl.ANY)
    return pl.pallas_call(
        functools.partial(image_kernel, tiles),
        out_shape=jax.ShapeDtypeStruct((2, per, tiles * inner), jnp.float32),
        in_specs=[vmem, pl.BlockSpec(memory_space=pltpu.SMEM), vmem, hbm, hbm, hbm],
        out_specs=vmem,
        scratch_shapes=[
            pltpu.VMEM(high.shape, jnp.bfloat16),
            pltpu.VMEM(low.shape, jnp.bfloat16),
            pltpu.VMEM(place.shape, jnp.bfloat16),
            pltpu.SemaphoreType.DMA((3,)),
        ],
        compiler_params=pltpu.CompilerParams(vmem_limit_bytes=62 * 1024 * 1024),
    )(grid, edges.T, twist, high, low, place)


def gegen_fix(field, edges):
    width = field.shape[-1]
    cells = jnp.arange(width, dtype=jnp.int32)[None, :]
    lower = edges[:, 0:1]
    upper = edges[:, 1:2]
    span = (upper - lower).astype(jnp.float32)
    inside = (cells >= lower) & (cells < upper)
    offset = (cells - lower).astype(jnp.float32)
    xi_vals = jnp.where(inside, -1.0 + (2.0 * offset + 1.0) / span, 0.0)
    base = 1.0 - xi_vals * xi_vals
    weight = jnp.where(inside, base * jnp.sqrt(base), 0.0)
    prev = jnp.ones_like(xi_vals)
    curr = 4.0 * xi_vals
    rebuilt = jnp.zeros_like(field)
    for order in range(GORDER):
        poly = prev if order == 0 else curr
        numer = jnp.sum(weight * poly * field, axis=-1)
        denom = jnp.sum(weight * poly * poly, axis=-1)
        rebuilt = rebuilt + (numer / denom)[..., None] * poly
        if order >= 1:
            nxt = (2.0 * (order + 2) * xi_vals * curr - (order + 3) * prev) / (order + 1)
            prev, curr = (curr, nxt)
    return jnp.where(inside, rebuilt, field)


def phase_table(first, second, modulus):
    left = jnp.arange(first, dtype=jnp.int32)[:, None]
    right = jnp.arange(second, dtype=jnp.int32)[None, :]
    angle = 2.0 * math.pi / modulus * (left * right % modulus).astype(jnp.float32)
    return (jnp.cos(angle), jnp.sin(angle))


def spectral(field, tiles):
    lines = field.shape[1]
    width = field.shape[2]
    inner = width // tiles
    blocks = field.reshape(2, lines, tiles, inner)
    real_part, imag_part = (blocks[0], blocks[1])
    best = lax.Precision.HIGHEST
    cos_outer, sin_outer = phase_table(tiles, tiles, tiles)
    g_real = jnp.einsum("pt,ctm->cpm", cos_outer, real_part, precision=best) - jnp.einsum(
        "pt,ctm->cpm", sin_outer, imag_part, precision=best
    )
    g_imag = jnp.einsum("pt,ctm->cpm", sin_outer, real_part, precision=best) + jnp.einsum(
        "pt,ctm->cpm", cos_outer, imag_part, precision=best
    )
    cos_twist, sin_twist = phase_table(tiles, inner, width)
    h_real = g_real * cos_twist - g_imag * sin_twist
    h_imag = g_real * sin_twist + g_imag * cos_twist
    cos_inner, sin_inner = phase_table(inner, inner, inner)
    z_real = jnp.einsum("qm,cpm->cqp", cos_inner, h_real, precision=best) - jnp.einsum(
        "qm,cpm->cqp", sin_inner, h_imag, precision=best
    )
    z_imag = jnp.einsum("qm,cpm->cqp", sin_inner, h_real, precision=best) + jnp.einsum(
        "qm,cpm->cqp", cos_inner, h_imag, precision=best
    )
    scale = 1.0 / math.sqrt(width)
    return jnp.stack([z_real, z_imag]).reshape(2, lines, width) * scale


def form_image_wide(grid, edges):
    chunks, tiles, _, per, piece = grid.shape
    inner = chunks * piece
    field = grid.transpose(2, 3, 1, 0, 4).reshape(2, per, tiles * inner)
    return gegen_fix(spectral(field, tiles), edges)


def on_device(sectors, footprint, own_blocks, edge_blocks, edges):
    grid = exchange(sectors[0], footprint[0], own_blocks, edge_blocks)
    if grid.shape[1] <= 8 and grid.shape[3] % 8 == 0:
        return form_image(grid, edges)
    return form_image_wide(grid, edges)


def solution(mesh):
    in_specs = (
        P("aperture", "tile", None, None, None),
        P("aperture", "tile", None),
        P(),
        P(),
        P(("aperture", "tile"), None),
    )
    out_specs = P(None, ("aperture", "tile"), None)
    return jax.shard_map(
        on_device, mesh=mesh, in_specs=in_specs, out_specs=out_specs, check_vma=False
    )
```

```python
import functools
import math

import jax
import jax.numpy as jnp
import ml_dtypes
import numpy as np
from jax import lax
from jax.experimental import pallas as pl
from jax.experimental.pallas import tpu as pltpu
from jax.sharding import PartitionSpec as P

GORDER = 8
MESH = pl.DeviceIdType.MESH


def partners(me, groups):
    if groups == 4:
        return [3 - me, lax.rem(me + 2, 4), me + 1 - 2 * lax.rem(me, 2)]
    return [lax.rem(me + step, groups) for step in range(1, groups)]


def exchange_kernel(
    groups, tiles, sec_ref, foot_ref, own_hbm, edge_hbm, out_ref,
    held, own_ref, edge_ref, wide, part, rims, rims_in, arrived, snd, rcv,
    load_sem, kern_sem, rim_send, rim_recv, rs_send, rs_recv, tr_send, tr_recv,
):
    slots, samples = sec_ref.shape[0], sec_ref.shape[1]
    blocks, piece = edge_ref.shape[0], edge_ref.shape[1]
    rows, width = part.shape[1], part.shape[2] // 2
    chunks = snd.shape[0]
    per = snd.shape[3]
    square = groups == 4
    me = lax.axis_index("aperture")
    tile = lax.axis_index("tile")
    flat = sec_ref.reshape(slots, 2 * samples, sec_ref.shape[3])
    others = partners(me, groups)
    order = others + [me]
    last = groups - 1

    def load(step):
        lanes = pl.ds(pl.multiple_of(order[step] * width, width), width)
        return pltpu.make_async_copy(flat.at[:, :, lanes], held.at[step], load_sem.at[step])

    kernels = [
        pltpu.make_async_copy(own_hbm, own_ref, kern_sem.at[0]),
        pltpu.make_async_copy(edge_hbm, edge_ref, kern_sem.at[1]),
    ]
    for copy in kernels:
        copy.start()
    for step in range(groups):
        load(step).start()

    barrier = pltpu.get_barrier_semaphore()
    greeted = others[1:] if square else others
    for other in greeted:
        pl.semaphore_signal(barrier, inc=1, device_id=(other, tile), device_id_type=MESH)
    for step in range(1, tiles):
        pl.semaphore_signal(barrier, inc=1, device_id=(me, lax.rem(tile + step, tiles)), device_id_type=MESH)
    pl.semaphore_wait(barrier, len(greeted) + tiles - 1)
    for copy in kernels:
        copy.wait()

    def span(chunk):
        return pl.ds(chunk * piece, piece)

    def rim_copy(step):
        return pltpu.make_async_remote_copy(
            src_ref=rims.at[step],
            dst_ref=rims_in.at[step],
            send_sem=rim_send.at[step],
            recv_sem=rim_recv.at[step],
            device_id=(me, lax.rem(tile + 1, tiles)),
            device_id_type=MESH,
        )

    def add_rim(step):
        @pl.when(tile > 0)
        def _():
            rim_copy(step).wait_recv()
            part[step, :piece] += rims_in[step]

    def reduce_copy(step, chunk):
        to = others[step]
        if square and step == 0:
            to = others[2 if chunk % 2 else 1]
        return pltpu.make_async_remote_copy(
            src_ref=part.at[step, span(chunk)],
            dst_ref=arrived.at[step, span(chunk)],
            send_sem=rs_send.at[step, chunk],
            recv_sem=rs_recv.at[step, chunk],
            device_id=(to, tile),
            device_id_type=MESH,
        )

    def relay(step, chunk):
        reduce_copy(0, chunk).wait_recv()
        part[step, span(chunk)] += arrived[0, span(chunk)]
        reduce_copy(step, chunk).start()

    for step in range(groups):
        load(step).wait()
        part[step] = jnp.zeros((rows, 2 * width), jnp.float32)
        rims[step] = jnp.zeros((piece, 2 * width), jnp.float32)

        @pl.loop(0, slots)
        def _(slot):
            wide[...] = held[step, slot].astype(jnp.float32)
            data = jnp.concatenate(
                [wide[pl.ds(0, samples, stride=2), :], wide[pl.ds(1, samples, stride=2), :]], axis=1
            ).astype(jnp.bfloat16)
            own, edge = foot_ref[0, slot], foot_ref[1, slot]
            whole = jnp.dot(own_ref[jnp.minimum(own, blocks - 1)], data, preferred_element_type=jnp.float32)
            rim = jnp.dot(edge_ref[jnp.minimum(edge, blocks - 1)], data, preferred_element_type=jnp.float32)
            part[step] += jnp.where(own < blocks, whole, 0.0)
            rims[step] += jnp.where(edge < blocks, rim, 0.0)

        @pl.when(tile < tiles - 1)
        def _():
            rim_copy(step).start()

        if not square:
            if step > 0:
                add_rim(step - 1)
                reduce_copy(step - 1, 0).start()
            if step < last:
                for chunk in range(1, chunks):
                    reduce_copy(step, chunk).start()
        elif step == 0:
            for chunk in range(1, chunks):
                reduce_copy(0, chunk).start()
        elif step == 1:
            add_rim(0)
            reduce_copy(0, 0).start()
            for chunk in range(2, chunks, 2):
                reduce_copy(1, chunk).start()
        elif step == 2:
            for chunk in range(1, chunks, 2):
                reduce_copy(2, chunk).start()
            for chunk in range(1, chunks, 2):
                relay(1, chunk)
            add_rim(1)
            reduce_copy(1, 0).start()
        else:
            for chunk in range(2, chunks, 2):
                relay(2, chunk)
            add_rim(2)
            relay(2, 0)

    def owner_copy(step, chunk):
        to = lax.rem(tile + step, tiles)
        return pltpu.make_async_remote_copy(
            src_ref=snd.at[chunk, to],
            dst_ref=rcv.at[chunk, tile],
            send_sem=tr_send.at[chunk, step],
            recv_sem=tr_recv.at[chunk, step],
            device_id=(me, to),
            device_id_type=MESH,
        )

    turn = list(range(1, chunks, 2)) + list(range(2, chunks, 2)) + [0]
    for chunk in turn:
        if chunk == 0:
            add_rim(last)
        total = part[last, span(chunk)]
        for step in range(1 if square else 0, last):
            reduce_copy(step, chunk).wait_recv()
            total = total + arrived[step, span(chunk)]
        for p in range(2):
            turned = total[:, p * width:(p + 1) * width].T
            for to in range(tiles):
                snd[chunk, to, p] = turned[to * per:(to + 1) * per]
        for step in range(1, tiles):
            owner_copy(step, chunk).start()
    for chunk in range(chunks):
        out_ref[chunk, tile] = snd[chunk, tile]
    for chunk in turn:
        for step in range(1, tiles):
            copy = owner_copy(step, chunk)
            copy.wait_send()
            copy.wait_recv()
            origin = lax.rem(tile + tiles - step, tiles)
            out_ref[chunk, origin] = rcv[chunk, origin]
    for step in range(last):
        for chunk in range(chunks):
            reduce_copy(step, chunk).wait_send()

    @pl.when(tile < tiles - 1)
    def _():
        for step in range(groups):
            rim_copy(step).wait_send()


def exchange(data, foot, own_blocks, edge_blocks):
    groups, tiles = lax.axis_size("aperture"), lax.axis_size("tile")
    slots, samples, _, lines = data.shape
    rows, piece = own_blocks.shape[1], edge_blocks.shape[1]
    width = lines // groups
    chunks, per = rows // piece, lines // (groups * tiles)
    out = (chunks, tiles, 2, per, piece)
    vmem = pl.BlockSpec(memory_space=pltpu.VMEM)
    hbm = pl.BlockSpec(memory_space=pl.ANY)
    return pl.pallas_call(
        functools.partial(exchange_kernel, groups, tiles),
        out_shape=jax.ShapeDtypeStruct(out, jnp.float32),
        in_specs=[hbm, pl.BlockSpec(memory_space=pltpu.SMEM), hbm, hbm],
        out_specs=vmem,
        scratch_shapes=[
            pltpu.VMEM((groups, slots, 2 * samples, width), jnp.bfloat16),
            pltpu.VMEM(own_blocks.shape, jnp.bfloat16),
            pltpu.VMEM(edge_blocks.shape, jnp.bfloat16),
            pltpu.VMEM((2 * samples, width), jnp.float32),
            pltpu.VMEM((groups, rows, 2 * width), jnp.float32),
            pltpu.VMEM((groups, piece, 2 * width), jnp.float32),
            pltpu.VMEM((groups, piece, 2 * width), jnp.float32),
            pltpu.VMEM((groups - 1, rows, 2 * width), jnp.float32),
            pltpu.VMEM(out, jnp.float32),
            pltpu.VMEM(out, jnp.float32),
            pltpu.SemaphoreType.DMA((groups,)),
            pltpu.SemaphoreType.DMA((2,)),
            pltpu.SemaphoreType.DMA((groups,)),
            pltpu.SemaphoreType.DMA((groups,)),
            pltpu.SemaphoreType.DMA((groups - 1, chunks)),
            pltpu.SemaphoreType.DMA((groups - 1, chunks)),
            pltpu.SemaphoreType.DMA((chunks, tiles)),
            pltpu.SemaphoreType.DMA((chunks, tiles)),
        ],
        compiler_params=pltpu.CompilerParams(
            collective_id=0, has_side_effects=True, vmem_limit_bytes=48 * 1024 * 1024
        ),
    )(data, foot.T, own_blocks, edge_blocks)


def split(value):
    high = value.astype(jnp.bfloat16)
    return high, (value - high.astype(jnp.float32)).astype(jnp.bfloat16)


def image_kernel(
    tiles, grid_ref, edges_ref, twist_ref, inner_high, inner_low, place_ref, out_ref
):
    per = edges_ref.shape[1]
    chunks, piece = grid_ref.shape[0], grid_ref.shape[4]
    inner = chunks * piece
    real, imag = [], []
    for t in range(tiles):
        for p, into in ((0, real), (1, imag)):
            into.append(jnp.concatenate([grid_ref[c, t, p] for c in range(chunks)], axis=1))
    h_real, h_imag = [], []
    for q in range(tiles):
        g_real, g_imag = real[0], imag[0]
        for t in range(1, tiles):
            angle = 2.0 * math.pi * (t * q % tiles) / tiles
            c, s = math.cos(angle), math.sin(angle)
            for factor, re, im in ((c, real[t], imag[t]), (s, -imag[t], real[t])):
                if abs(factor) < 1e-12:
                    continue
                if abs(abs(factor) - 1.0) < 1e-12:
                    g_real = g_real + re if factor > 0 else g_real - re
                    g_imag = g_imag + im if factor > 0 else g_imag - im
                else:
                    g_real = g_real + factor * re
                    g_imag = g_imag + factor * im
        c, s = twist_ref[0, q:q + 1, :], twist_ref[1, q:q + 1, :]
        h_real.append(g_real * c - g_imag * s)
        h_imag.append(g_real * s + g_imag * c)
    stacked = jnp.concatenate(h_real + h_imag, axis=0)
    high, low = split(stacked)
    both = jnp.concatenate([high, low], axis=0)
    dot = functools.partial(jnp.dot, preferred_element_type=jnp.float32)
    count = tiles * per

    def times(index):
        wide = dot(both, inner_high[index])
        return wide[:2 * count] + wide[2 * count:] + dot(high, inner_low[index])

    by_cos, by_sin = times(0), times(1)
    z_real = (by_cos[:count] - by_sin[count:]).reshape(tiles, per, inner)
    z_imag = (by_sin[:count] + by_cos[count:]).reshape(tiles, per, inner)

    line = lax.broadcasted_iota(jnp.int32, (1, per, 1), 1)
    lower = upper = jnp.zeros((1, per, 1), jnp.int32)
    for at in range(per):
        lower = jnp.where(line == at, edges_ref[0, at], lower)
        upper = jnp.where(line == at, edges_ref[1, at], upper)
    shape = (tiles, per, inner)
    cells = lax.broadcasted_iota(jnp.int32, shape, 2) * tiles + lax.broadcasted_iota(jnp.int32, shape, 0)
    inside = (cells >= lower) & (cells < upper)
    span = (upper - lower).astype(jnp.float32)
    offset = (cells - lower).astype(jnp.float32)
    xi = jnp.where(inside, -1.0 + (2.0 * offset + 1.0) / span, 0.0)
    base = 1.0 - xi * xi
    weight = jnp.where(inside, base * jnp.sqrt(base), 0.0)

    def over_line(value):
        return jnp.sum(jnp.sum(value, axis=0), axis=-1, keepdims=True)[None]

    prev, curr = jnp.ones_like(xi), 4.0 * xi
    re_fix, im_fix = jnp.zeros_like(xi), jnp.zeros_like(xi)
    for order in range(GORDER):
        poly = prev if order == 0 else curr
        weighted = weight * poly
        denom = over_line(weighted * poly)
        re_fix = re_fix + (over_line(weighted * z_real) / denom) * poly
        im_fix = im_fix + (over_line(weighted * z_imag) / denom) * poly
        if order >= 1:
            nxt = xi * curr * (2.0 * (order + 2) / (order + 1)) - prev * ((order + 3) / (order + 1))
            prev, curr = curr, nxt
    fixed = (jnp.where(inside, re_fix, z_real), jnp.where(inside, im_fix, z_imag))

    lanes = 128
    strips = inner // lanes
    lines = []
    for strip in range(strips):
        for value in fixed:
            lines.append(
                jnp.concatenate([value[q, :, strip * lanes:(strip + 1) * lanes] for q in range(tiles)], axis=1)
            )
    high, low = split(jnp.concatenate(lines, axis=0))
    placed = dot(jnp.concatenate([high, low], axis=0), place_ref[...])
    placed = placed[:strips * 2 * per] + placed[strips * 2 * per:]
    for strip in range(strips):
        for p in range(2):
            at = (strip * 2 + p) * per
            out_ref[p, :, strip * lanes * tiles:(strip + 1) * lanes * tiles] = placed[at:at + per]


def tables(tiles, inner):
    width = tiles * inner
    twist = 2.0 * np.pi * np.outer(np.arange(tiles), np.arange(inner)) / width
    twist = np.stack([np.cos(twist), np.sin(twist)]) / math.sqrt(width)
    angle = 2.0 * np.pi * (np.outer(np.arange(inner), np.arange(inner)) % inner) / inner
    table = np.stack([np.cos(angle), np.sin(angle)]).astype(np.float32)
    high = table.astype(ml_dtypes.bfloat16)
    low = (table - high.astype(np.float32)).astype(ml_dtypes.bfloat16)
    lanes = 128
    place = np.zeros((tiles, lanes, lanes * tiles), np.float32)
    for q in range(tiles):
        place[q, np.arange(lanes), np.arange(lanes) * tiles + q] = 1.0
    place = place.reshape(tiles * lanes, lanes * tiles).astype(ml_dtypes.bfloat16)
    return twist.astype(np.float32), high, low, place


def form_image(grid, edges):
    chunks, tiles, _, per, piece = grid.shape
    inner = chunks * piece
    twist, high, low, place = tables(tiles, inner)
    vmem = pl.BlockSpec(memory_space=pltpu.VMEM)
    return pl.pallas_call(
        functools.partial(image_kernel, tiles),
        out_shape=jax.ShapeDtypeStruct((2, per, tiles * inner), jnp.float32),
        in_specs=[vmem, pl.BlockSpec(memory_space=pltpu.SMEM)] + [vmem] * 4,
        out_specs=vmem,
        compiler_params=pltpu.CompilerParams(vmem_limit_bytes=40 * 1024 * 1024),
    )(grid, edges.T, twist, high, low, place)


def gegen_fix(field, edges):
    width = field.shape[-1]
    cells = jnp.arange(width, dtype=jnp.int32)[None, :]
    lower = edges[:, 0:1]
    upper = edges[:, 1:2]
    span = (upper - lower).astype(jnp.float32)
    inside = (cells >= lower) & (cells < upper)
    offset = (cells - lower).astype(jnp.float32)
    xi_vals = jnp.where(inside, -1.0 + (2.0 * offset + 1.0) / span, 0.0)
    base = 1.0 - xi_vals * xi_vals
    weight = jnp.where(inside, base * jnp.sqrt(base), 0.0)
    prev = jnp.ones_like(xi_vals)
    curr = 4.0 * xi_vals
    rebuilt = jnp.zeros_like(field)
    for order in range(GORDER):
        poly = prev if order == 0 else curr
        numer = jnp.sum(weight * poly * field, axis=-1)
        denom = jnp.sum(weight * poly * poly, axis=-1)
        rebuilt = rebuilt + (numer / denom)[..., None] * poly
        if order >= 1:
            nxt = (2.0 * (order + 2) * xi_vals * curr - (order + 3) * prev) / (order + 1)
            prev, curr = (curr, nxt)
    return jnp.where(inside, rebuilt, field)


def phase_table(first, second, modulus):
    left = jnp.arange(first, dtype=jnp.int32)[:, None]
    right = jnp.arange(second, dtype=jnp.int32)[None, :]
    angle = 2.0 * math.pi / modulus * (left * right % modulus).astype(jnp.float32)
    return (jnp.cos(angle), jnp.sin(angle))


def spectral(field, tiles):
    lines = field.shape[1]
    width = field.shape[2]
    inner = width // tiles
    blocks = field.reshape(2, lines, tiles, inner)
    real_part, imag_part = (blocks[0], blocks[1])
    best = lax.Precision.HIGHEST
    cos_outer, sin_outer = phase_table(tiles, tiles, tiles)
    g_real = jnp.einsum("pt,ctm->cpm", cos_outer, real_part, precision=best) - jnp.einsum(
        "pt,ctm->cpm", sin_outer, imag_part, precision=best
    )
    g_imag = jnp.einsum("pt,ctm->cpm", sin_outer, real_part, precision=best) + jnp.einsum(
        "pt,ctm->cpm", cos_outer, imag_part, precision=best
    )
    cos_twist, sin_twist = phase_table(tiles, inner, width)
    h_real = g_real * cos_twist - g_imag * sin_twist
    h_imag = g_real * sin_twist + g_imag * cos_twist
    cos_inner, sin_inner = phase_table(inner, inner, inner)
    z_real = jnp.einsum("qm,cpm->cqp", cos_inner, h_real, precision=best) - jnp.einsum(
        "qm,cpm->cqp", sin_inner, h_imag, precision=best
    )
    z_imag = jnp.einsum("qm,cpm->cqp", sin_inner, h_real, precision=best) + jnp.einsum(
        "qm,cpm->cqp", cos_inner, h_imag, precision=best
    )
    scale = 1.0 / math.sqrt(width)
    return jnp.stack([z_real, z_imag]).reshape(2, lines, width) * scale


def form_image_wide(grid, edges):
    chunks, tiles, _, per, piece = grid.shape
    inner = chunks * piece
    field = grid.transpose(2, 3, 1, 0, 4).reshape(2, per, tiles * inner)
    return gegen_fix(spectral(field, tiles), edges)


def on_device(sectors, footprint, own_blocks, edge_blocks, edges):
    grid = exchange(sectors[0], footprint[0], own_blocks, edge_blocks)
    if grid.shape[1] <= 8 and grid.shape[3] % 8 == 0:
        return form_image(grid, edges)
    return form_image_wide(grid, edges)


def solution(mesh):
    in_specs = (
        P("aperture", "tile", None, None, None),
        P("aperture", "tile", None),
        P(),
        P(),
        P(("aperture", "tile"), None),
    )
    out_specs = P(None, ("aperture", "tile"), None)
    return jax.shard_map(
        on_device, mesh=mesh, in_specs=in_specs, out_specs=out_specs, check_vma=False
    )
```
